32 devices in a mesh: pb: 4 (over y, x), ga: 8 (over z, core).
Axes of the slice: x: 2, y: 2, z: 4, core: 2. Of those that a mesh axis runs over, the one named last changes fastest.
Arguments:
- valence: bfloat16 [24, 4, 16, 768], P('pb', None, None, 'ga'), may hold values from -6 to 6
- conduction: bfloat16 [24, 4, 8, 768], P('pb', None, None, 'ga'), may hold values from -6 to 6
- screened: bfloat16 [4, 768, 768], P('pb', 'ga'), as said below
- kq_table: int32 [24, 4], P('pb'), may hold values from 0 to 3, each once within a row
Outputs:
- kernel: float32 [24, 4, 8, 16], P('pb')
The draws below stay inside these ranges and needn't reach their ends.
Inputs may be any that keep to these rules, and one draw needn't show every extreme that they name: screened is symmetric in its last two dimensions: screened[q, G, H] = screened[q, H, G] exactly. Each row of kq_table names every label of 0 to 3 once.
All inputs are finite; a program needn't handle non-finite values.
Results may differ from the reference program's by a relative error of at most 0.0003.
Values may be sent and summed in bfloat16 or wider, within the bound.
No kernel may reach another device: no remote copies, remote signals or barrier semaphores. Data moves between devices by JAX's collectives and lax.ppermute only.
A program may use at most 128 MiB of HBM per device.

```python
import math
import jax
import jax.numpy as jnp
from jax import lax

NPV = 16
NPC = 8
NG = 768
NK = 24
NQ = 4


def draw_screened(key, part):
    key_raw = jax.random.fold_in(key, 11)
    key_diag = jax.random.fold_in(key, 12)
    key_scale = jax.random.fold_in(key, 13)
    raw = jnp.clip(jax.random.normal(key_raw, (NQ, NG, NG), jnp.float32), -4.0, 4.0)
    scales = jnp.exp(jax.random.uniform(key_scale, (NQ, NG), jnp.float32, math.log(0.7), math.log(1.4)))
    diag_vals = jnp.exp(jax.random.uniform(key_diag, (NQ, NG), jnp.float32, 0.0, math.log(4.0))) / math.sqrt(NG)
    sym_part = 0.5 * (raw + jnp.swapaxes(raw, 1, 2)) / NG
    row_ids = jnp.arange(NG)[:, None]
    col_ids = jnp.arange(NG)[None, :]
    core = jnp.where(row_ids == col_ids, diag_vals[:, :, None], sym_part)
    outer = scales[:, :, None] * scales[:, None, :]
    return (outer * core).astype(jnp.bfloat16)


def block_scale(key, shape, shards, least, top_value):
    gain = 1.0
    for axis_at, parts in shards:
        steps = jax.random.uniform(jax.random.fold_in(jax.random.fold_in(key, 6), axis_at), (parts,), jnp.float32, least / len(shards), top_value / len(shards))
        gain = gain * jnp.repeat(jnp.exp(steps), shape[axis_at] // parts).reshape((-1,) + (1,) * (len(shape) - 1 - axis_at))
    return gain


def centred(own_key, shape, width, most, cuts=(), kind=jnp.bfloat16):
    array = width * jax.random.normal(own_key, shape, jnp.float32)
    if cuts:
        array = array * block_scale(own_key, shape, cuts, -0.22, 0.18)
    return jnp.clip(array, -most, most).astype(kind)


def setup_inputs(seed: int = 0) -> dict:
    key_of = jax.random.split(jax.random.key(seed), 5)
    valence = centred(key_of[0], (NK, NQ, NPV, NG), 1.0, 6.0, ((0, 4), (3, 8)))
    conduction = centred(key_of[1], (NK, NQ, NPC, NG), 1.0, 6.0, ((0, 4), (3, 8)))
    screened = draw_screened(jax.random.fold_in(key_of[4], 71), 0)
    kq_table = jax.vmap(lambda own: jax.random.permutation(own, NQ))(jax.random.split(key_of[3], NK)).reshape((NK, NQ)).astype(jnp.int32)
    return {"valence": valence, "conduction": conduction, "screened": screened, "kq_table": kq_table}


def one_point(operands):
    w_rows, val_part, con_part = operands
    applied = jnp.einsum("gh,kvh->kvg", w_rows.astype(jnp.float32), val_part.astype(jnp.float32), precision=lax.Precision.HIGHEST)
    return jnp.einsum("kcg,kvg->kcv", con_part.astype(jnp.float32), applied, precision=lax.Precision.HIGHEST)


def reference(valence, conduction, screened, kq_table):
    blocks = lax.map(one_point, (screened, jnp.moveaxis(valence, 1, 0), jnp.moveaxis(conduction, 1, 0)))
    blocks = jnp.moveaxis(blocks, 0, 1)
    k_rows = jnp.arange(NK, dtype=jnp.int32)[:, None]
    kernel = jnp.zeros((NK, NQ, NPC, NPV), jnp.float32).at[k_rows, kq_table].set(blocks)
    return kernel
```

```python
import functools

import jax
import jax.numpy as jnp
from jax import lax
from jax.experimental import pallas as pl
from jax.experimental.pallas import tpu as pltpu
from jax.sharding import PartitionSpec as P

CORES = 2
LANES = 128


def partner(i, s, n):
    return i ^ s if n & (n - 1) == 0 else (i + s) % n


def source(i, s, n):
    return jnp.bitwise_xor(i, s) if n & (n - 1) == 0 else lax.rem(i + (n - s), n)


def send_pb(x, s, npb):
    return lax.ppermute(x, "pb", [(i, partner(i, s, npb)) for i in range(npb)])


def send_chip(x, s, nz):
    return lax.ppermute(
        x,
        "ga",
        [(i * CORES + c, partner(i, s, nz) * CORES + c) for i in range(nz) for c in range(CORES)],
    )


def send_core(x, nz):
    return lax.ppermute(
        x, "ga", [(i * CORES + c, i * CORES + 1 - c) for i in range(nz) for c in range(CORES)]
    )


def dot_nt(a, b):
    return lax.dot_general(a, b, (((1,), (1,)), ((), ())), preferred_element_type=jnp.float32)


def partial_kernel(npb, nz, *refs):
    w_refs, mine_refs = refs[:npb], refs[npb : npb + nz]
    other_ref, val_ref, out_ref, slab_ref, full_ref = refs[npb + nz :]
    nk, nq, nc, ng = mine_refs[0].shape
    nv = val_ref.shape[2]
    per_tile = LANES // nv
    pb, ga = lax.axis_index("pb"), lax.axis_index("ga")
    z, core = lax.div(ga, CORES), lax.rem(ga, CORES)
    for s in range(nz):
        first = source(z, s, nz) * CORES
        slab_ref[first + core] = mine_refs[s][...]
        slab_ref[first + 1 - core] = other_ref[s]
    lane_block = lax.broadcasted_iota(jnp.int32, (nc, LANES), 1) // nv
    tiles = [jnp.zeros((nc, LANES), jnp.float32) for _ in range(out_ref.shape[0])]

    def join(q, _):
        for p in range(nz * CORES):
            piece = slab_ref[p, :, q].astype(jnp.float32).reshape(nk * nc, ng)
            full_ref[q, :, p * ng : (p + 1) * ng] = piece.astype(jnp.bfloat16)

    lax.fori_loop(0, nq, join, None, unroll=min(nq, 4))
    for s in range(npb):
        q = source(pb, s, npb)
        applied = dot_nt(full_ref[q], w_refs[s][0])
        high = applied.astype(jnp.bfloat16)
        low = (applied - high.astype(jnp.float32)).astype(jnp.bfloat16)
        val = val_ref[:, q].astype(jnp.float32).reshape(nk * nv, ng).astype(jnp.bfloat16)
        val = jnp.concatenate([val, jnp.zeros((LANES - nk * nv, ng), jnp.bfloat16)], axis=0)
        product = dot_nt(high, val) + dot_nt(low, val)
        for k in range(nk):
            tile, place = divmod(k * npb + s, per_tile)
            moved = pltpu.roll(
                product[k * nc : (k + 1) * nc], ((place - k) * nv) % LANES, axis=1
            )
            tiles[tile] = jnp.where(lane_block == place, moved, tiles[tile])
    for t, tile in enumerate(tiles):
        out_ref[t] = tile


def place_kernel(npb, nz, *refs):
    share_refs, (kq_ref, out_ref) = refs[:nz], refs[nz:]
    nk, _, _, nv = out_ref.shape
    per_tile = LANES // nv
    pb = lax.axis_index("pb")
    total = share_refs[0][...]
    for share_ref in share_refs[1:]:
        total = total + share_ref[...]
    for s in range(npb):
        q = source(pb, s, npb)
        for k in range(nk):
            tile, place = divmod(k * npb + s, per_tile)
            out_ref[k, kq_ref[k, q]] = total[tile, :, place * nv : (place + 1) * nv]


def per_device(npb, nz, valence, conduction, screened, kq_table):
    nk, nq, nv, ng = valence.shape
    nc = conduction.shape[2]
    vmem = pl.BlockSpec(memory_space=pltpu.VMEM)
    smem = pl.BlockSpec(memory_space=pltpu.SMEM)

    w_parts = [screened] + [send_pb(screened, s, npb) for s in range(1, npb)]
    mine = [conduction] + [send_chip(conduction, s, nz) for s in range(1, nz)]
    other = send_core(jnp.stack(mine), nz)
    n_tiles = -(-nk * nq * nv // LANES)
    partial_value = pl.pallas_call(
        functools.partial(partial_kernel, npb, nz),
        out_shape=jax.ShapeDtypeStruct((n_tiles, nc, LANES), jnp.float32),
        in_specs=[vmem] * (npb + nz + 2),
        out_specs=vmem,
        scratch_shapes=[
            pltpu.VMEM((nz * CORES, nk, nq, nc, ng), jnp.bfloat16),
            pltpu.VMEM((nq, nk * nc, nz * CORES * ng), jnp.bfloat16),
        ],
        compiler_params=pltpu.CompilerParams(vmem_limit_bytes=48 * 2**20),
    )(*w_parts, *mine, other, valence)
    chip_value = partial_value + send_core(partial_value, nz)
    shares = [chip_value] + [send_chip(chip_value, s, nz) for s in range(1, nz)]
    return pl.pallas_call(
        functools.partial(place_kernel, npb, nz),
        out_shape=jax.ShapeDtypeStruct((nk, nq, nc, nv), jnp.float32),
        in_specs=[vmem] * nz + [smem],
        out_specs=vmem,
    )(*shares, kq_table)


def solution(mesh):
    npb, nga = mesh.shape["pb"], mesh.shape["ga"]
    return jax.shard_map(
        functools.partial(per_device, npb, nga // CORES),
        mesh=mesh,
        in_specs=(
            P("pb", None, None, "ga"),
            P("pb", None, None, "ga"),
            P("pb", "ga", None),
            P("pb", None),
        ),
        out_specs=P("pb", None, None, None),
        check_vma=False,
    )
```

```python
import functools
import math

import jax
import jax.numpy as jnp
from jax import lax
from jax.experimental import pallas as pl
from jax.experimental.pallas import tpu as pltpu
from jax.sharding import PartitionSpec as P

CORES = 2
LANES = 128
VMEM_LIMIT = 24 * 2**20


def partner(i, s, n):
    return i ^ s if n & (n - 1) == 0 else (i + s) % n


def source(i, s, n):
    return jnp.bitwise_xor(i, s) if n & (n - 1) == 0 else lax.rem(i + (n - s), n)


def send_pb(x, s, npb):
    return lax.ppermute(x, "pb", [(i, partner(i, s, npb)) for i in range(npb)])


def send_chip(x, s, nz):
    return lax.ppermute(
        x,
        "ga",
        [(i * CORES + c, partner(i, s, nz) * CORES + c) for i in range(nz) for c in range(CORES)],
    )


def chip_stages(nz):
    stages, stride = [], nz
    while stride > 1:
        size = next(f for f in range(2, stride + 1) if stride % f == 0)
        stride //= size
        stages.append((stride, size))
    return stages


def shift_digit(i, s, stride, size):
    digit = i // stride % size
    return i + ((digit + s) % size - digit) * stride


def gather_chips(x, nz):
    shifts, parts = [()], [x[None]]
    for stride, size in chip_stages(nz):
        held = parts[0] if len(parts) == 1 else jnp.concatenate(parts)
        parts = [held]
        old = shifts
        for s in range(1, size):
            pairs = [
                (i * CORES + c, shift_digit(i, s, stride, size) * CORES + c)
                for i in range(nz)
                for c in range(CORES)
            ]
            parts.append(lax.ppermute(held, "ga", pairs))
            shifts = shifts + [was + ((stride, size, size - s),) for was in old]
    return parts, shifts


def apply_shifts(z, path):
    for stride, size, s in path:
        digit = lax.rem(lax.div(z, stride), size)
        z = z + (lax.rem(digit + s, size) - digit) * stride
    return z


def send_core(x, nz):
    return lax.ppermute(
        x, "ga", [(i * CORES + c, i * CORES + 1 - c) for i in range(nz) for c in range(CORES)]
    )


def dot_nt(a, b):
    return lax.dot_general(a, b, (((1,), (1,)), ((), ())), preferred_element_type=jnp.float32)


def pack_kernel(con_ref, out_ref):
    nk, nq, nc, ng = con_ref.shape
    for q in range(nq):
        rows = con_ref[:, q].astype(jnp.float32).reshape(nk * nc, ng)
        out_ref[:, q * ng : (q + 1) * ng] = rows.astype(jnp.bfloat16)


def join_slabs(shifts, core, part_refs, slab_ref, full_ref):
    nz = len(shifts)
    ng = full_ref.shape[2] // (nz * CORES)
    z = lax.div(lax.axis_index("ga"), CORES)
    pieces = [ref.at[i] for ref in part_refs for i in range(ref.shape[0])]
    for path, piece in zip(shifts, pieces):
        first = apply_shifts(z, path) * CORES
        slab_ref[first + core] = piece[...]
        slab_ref[first + 1 - core] = jnp.zeros(slab_ref.shape[1:], jnp.bfloat16)
    n_slabs, nq = nz * CORES, full_ref.shape[0]
    group = LANES // math.gcd(ng, LANES)
    slab_group = group if n_slabs % group == 0 else n_slabs
    q_group = group if nq % group == 0 else nq
    n_steps = (n_slabs // slab_group) * (nq // q_group)

    def join(step, _):
        p0 = lax.rem(step, n_slabs // slab_group) * slab_group
        q0 = lax.div(step, n_slabs // slab_group) * q_group
        loaded = [
            slab_ref[p0 + p, :, pl.ds(pl.multiple_of(q0 * ng, q_group * ng), q_group * ng)]
            for p in range(slab_group)
        ]
        for q in range(q_group):
            row = [x[:, q * ng : (q + 1) * ng] for x in loaded]
            full_ref[
                q0 + q, :, pl.ds(pl.multiple_of(p0 * ng, slab_group * ng), slab_group * ng)
            ] = jnp.concatenate(row, axis=1)

    lax.fori_loop(0, n_steps, join, None, unroll=n_steps <= 4)


def near_kernel(npb, shifts, *refs):
    w_refs, part_refs = refs[:npb], refs[npb:-3]
    out_ref, slab_ref, full_ref = refs[-3:]
    pb, ga = lax.axis_index("pb"), lax.axis_index("ga")
    join_slabs(shifts, lax.rem(ga, CORES), part_refs, slab_ref, full_ref)
    for s in range(npb):
        out_ref[s] = dot_nt(full_ref[source(pb, s, npb)], w_refs[s][0])


def partial_kernel(npb, shifts, *refs):
    w_refs, part_refs = refs[:npb], refs[npb:-5]
    near_ref, val_ref, out_ref, slab_ref, full_ref = refs[-5:]
    nk, _, nv, ng = val_ref.shape
    nc = near_ref.shape[1] // nk
    per_tile = LANES // nv
    pb, ga = lax.axis_index("pb"), lax.axis_index("ga")
    join_slabs(shifts, 1 - lax.rem(ga, CORES), part_refs, slab_ref, full_ref)
    lane_block = lax.broadcasted_iota(jnp.int32, (nc, LANES), 1) // nv
    tiles = [jnp.zeros((nc, LANES), jnp.float32) for _ in range(out_ref.shape[0])]
    for s in range(npb):
        q = source(pb, s, npb)
        applied = near_ref[s] + dot_nt(full_ref[q], w_refs[s][0])
        high = applied.astype(jnp.bfloat16)
        low = (applied - high.astype(jnp.float32)).astype(jnp.bfloat16)
        val = val_ref[:, q].astype(jnp.float32).reshape(nk * nv, ng).astype(jnp.bfloat16)
        val = jnp.concatenate([val, jnp.zeros((LANES - nk * nv, ng), jnp.bfloat16)], axis=0)
        product = dot_nt(high, val) + dot_nt(low, val)
        for k in range(nk):
            tile, place = divmod(k * npb + s, per_tile)
            moved = pltpu.roll(
                product[k * nc : (k + 1) * nc], ((place - k) * nv) % LANES, axis=1
            )
            tiles[tile] = jnp.where(lane_block == place, moved, tiles[tile])
    for t, tile in enumerate(tiles):
        out_ref[t] = tile


def place_kernel(npb, nz, *refs):
    share_refs, (kq_ref, out_ref) = refs[:nz], refs[nz:]
    nk, _, _, nv = out_ref.shape
    per_tile = LANES // nv
    pb = lax.axis_index("pb")
    total = share_refs[0][...]
    for share_ref in share_refs[1:]:
        total = total + share_ref[...]
    for s in range(npb):
        q = source(pb, s, npb)
        for k in range(nk):
            tile, place = divmod(k * npb + s, per_tile)
            out_ref[k, kq_ref[q, k]] = total[tile, :, place * nv : (place + 1) * nv]


def per_device(npb, nz, valence, conduction, screened, kq_table):
    nk, nq, nv, ng = valence.shape
    nc = conduction.shape[2]
    vmem = pl.BlockSpec(memory_space=pltpu.VMEM)
    smem = pl.BlockSpec(memory_space=pltpu.SMEM)
    params = pltpu.CompilerParams(vmem_limit_bytes=VMEM_LIMIT)
    join_scratch = [
        pltpu.VMEM((nz * CORES, nk * nc, nq * ng), jnp.bfloat16),
        pltpu.VMEM((nq, nk * nc, nz * CORES * ng), jnp.bfloat16),
    ]

    w_parts = [screened] + [send_pb(screened, s, npb) for s in range(1, npb)]
    packed = pl.pallas_call(
        pack_kernel,
        out_shape=jax.ShapeDtypeStruct((nk * nc, nq * ng), jnp.bfloat16),
        in_specs=[vmem],
        out_specs=vmem,
        compiler_params=params,
        cost_estimate=pl.CostEstimate(flops=0, bytes_accessed=1000000, transcendentals=0),
    )(conduction)
    mine, shifts = gather_chips(packed, nz)
    other = [send_core(part, nz) for part in mine]
    near = pl.pallas_call(
        functools.partial(near_kernel, npb, shifts),
        out_shape=jax.ShapeDtypeStruct((npb, nk * nc, ng), jnp.float32),
        in_specs=[vmem] * (npb + len(mine)),
        out_specs=vmem,
        scratch_shapes=join_scratch,
        compiler_params=params,
        cost_estimate=pl.CostEstimate(
            flops=2 * nk * nq * nc * ng * ng * nz, bytes_accessed=3000000, transcendentals=0
        ),
    )(*w_parts, *mine)
    n_tiles = -(-nk * nq * nv // LANES)
    partial_value = pl.pallas_call(
        functools.partial(partial_kernel, npb, shifts),
        out_shape=jax.ShapeDtypeStruct((n_tiles, nc, LANES), jnp.float32),
        in_specs=[vmem] * (npb + len(mine) + 2),
        out_specs=vmem,
        scratch_shapes=join_scratch,
        compiler_params=params,
    )(*w_parts, *other, near, valence)
    chip_value = partial_value + send_core(partial_value, nz)
    shares = [chip_value] + [send_chip(chip_value, s, nz) for s in range(1, nz)]
    return pl.pallas_call(
        functools.partial(place_kernel, npb, nz),
        out_shape=jax.ShapeDtypeStruct((nk, nq, nc, nv), jnp.float32),
        in_specs=[vmem] * nz + [smem],
        out_specs=vmem,
        compiler_params=params,
    )(*shares, kq_table.T)


def solution(mesh):
    npb, nga = mesh.shape["pb"], mesh.shape["ga"]
    return jax.shard_map(
        functools.partial(per_device, npb, nga // CORES),
        mesh=mesh,
        in_specs=(
            P("pb", None, None, "ga"),
            P("pb", None, None, "ga"),
            P("pb", "ga", None),
            P("pb", None),
        ),
        out_specs=P("pb", None, None, None),
        check_vma=False,
    )
```

```python
import functools
import math

import jax
import jax.numpy as jnp
from jax import lax
from jax.experimental import pallas as pl
from jax.experimental.pallas import tpu as pltpu
from jax.sharding import PartitionSpec as P

CORES = 2
LANES = 128
VMEM_LIMIT = 24 * 2**20


def partner(i, s, n):
    return i ^ s if n & (n - 1) == 0 else (i + s) % n


def source(i, s, n):
    return jnp.bitwise_xor(i, s) if n & (n - 1) == 0 else lax.rem(i + (n - s), n)


def send_pb(x, s, npb):
    return lax.ppermute(x, "pb", [(i, partner(i, s, npb)) for i in range(npb)])


def send_chip(x, s, nz):
    return lax.ppermute(
        x,
        "ga",
        [(i * CORES + c, partner(i, s, nz) * CORES + c) for i in range(nz) for c in range(CORES)],
    )


def chip_stages(nz):
    stages, stride = [], nz
    while stride > 1:
        size = next(f for f in range(2, stride + 1) if stride % f == 0)
        stride //= size
        stages.append((stride, size))
    return stages


def shift_digit(i, s, stride, size):
    digit = i // stride % size
    return i + ((digit + s) % size - digit) * stride


def gather_chips(x, nz, join):
    shifts, parts = [()], [x]
    for i, (stride, size) in enumerate(chip_stages(nz)):
        held = x
        if i:
            held = join(*parts) if i == 1 else jnp.concatenate(parts)
        parts = [held]
        old = shifts
        for s in range(1, size):
            pairs = [
                (i * CORES + c, shift_digit(i, s, stride, size) * CORES + c)
                for i in range(nz)
                for c in range(CORES)
            ]
            parts.append(lax.ppermute(held, "ga", pairs))
            shifts = shifts + [was + ((stride, size, size - s),) for was in old]
    return parts, shifts


def apply_shifts(z, path):
    for stride, size, s in path:
        digit = lax.rem(lax.div(z, stride), size)
        z = z + (lax.rem(digit + s, size) - digit) * stride
    return z


def send_core(x, nz):
    return lax.ppermute(
        x, "ga", [(i * CORES + c, i * CORES + 1 - c) for i in range(nz) for c in range(CORES)]
    )


def dot_nt(a, b):
    return lax.dot_general(a, b, (((1,), (1,)), ((), ())), preferred_element_type=jnp.float32)


def pack(con_ref, out_ref):
    nk, nq, nc, ng = con_ref.shape
    for q in range(nq):
        rows = con_ref[:, q].astype(jnp.float32).reshape(nk * nc, ng)
        out_ref[:, q * ng : (q + 1) * ng] = rows.astype(jnp.bfloat16)


def pack_kernel(own_ref, *refs):
    out_ref = refs[-1]
    out_ref[0] = own_ref[...]
    for i, con_ref in enumerate(refs[:-1]):
        pack(con_ref, out_ref.at[i + 1])


def prepare_kernel(npb, held_ref, val_ref, kq_ref, sent_ref, out_ref):
    nk, nq, nv, ng = val_ref.shape
    per_tile = LANES // nv
    pb = lax.axis_index("pb")
    sent_ref[...] = held_ref[...]
    out_ref[...] = jnp.zeros(out_ref.shape, out_ref.dtype)
    for s in range(npb):
        q = source(pb, s, npb)
        for k in range(nk):
            block = k * nq + kq_ref[q, k]
            rows = pl.ds(pl.multiple_of(lax.rem(block, per_tile) * nv, nv), nv)
            out_ref[lax.div(block, per_tile), rows, s * LANES : s * LANES + ng] = val_ref[k, q]


def join_slabs(shifts, core, part_refs, slab_ref, full_ref):
    nz = len(shifts)
    ng = full_ref.shape[2] // (nz * CORES)
    z = lax.div(lax.axis_index("ga"), CORES)
    pieces = [ref.at[i] for ref in part_refs for i in range(ref.shape[0])]
    for path, piece in zip(shifts, pieces):
        first = apply_shifts(z, path) * CORES
        slab_ref[first + core] = piece[...]
        slab_ref[first + 1 - core] = jnp.zeros(slab_ref.shape[1:], jnp.bfloat16)
    n_slabs, nq = nz * CORES, full_ref.shape[0]
    group = LANES // math.gcd(ng, LANES)
    slab_group = group if n_slabs % group == 0 else n_slabs
    q_group = group if nq % group == 0 else nq
    n_steps = (n_slabs // slab_group) * (nq // q_group)

    def join(step, _):
        p0 = lax.rem(step, n_slabs // slab_group) * slab_group
        q0 = lax.div(step, n_slabs // slab_group) * q_group
        loaded = [
            slab_ref[p0 + p, :, pl.ds(pl.multiple_of(q0 * ng, q_group * ng), q_group * ng)]
            for p in range(slab_group)
        ]
        for q in range(q_group):
            row = [x[:, q * ng : (q + 1) * ng] for x in loaded]
            full_ref[
                q0 + q, :, pl.ds(pl.multiple_of(p0 * ng, slab_group * ng), slab_group * ng)
            ] = jnp.concatenate(row, axis=1)

    lax.fori_loop(0, n_steps, join, None, unroll=n_steps <= 4)


def near_kernel(npb, shifts, *refs):
    w_refs, part_refs = refs[:npb], refs[npb:-3]
    out_ref, slab_ref, full_ref = refs[-3:]
    pb, ga = lax.axis_index("pb"), lax.axis_index("ga")
    join_slabs(shifts, lax.rem(ga, CORES), part_refs, slab_ref, full_ref)
    for s in range(npb):
        out_ref[s] = dot_nt(full_ref[source(pb, s, npb)], w_refs[s][0])


def partial_kernel(npb, shifts, *refs):
    w_refs, part_refs = refs[:npb], refs[npb:-5]
    near_ref, val_ref, out_ref, slab_ref, full_ref = refs[-5:]
    n_tiles, nc, _ = out_ref.shape
    nq, rows, ng = near_ref.shape
    nk = rows // nc
    blocks = nk * nq // n_tiles
    pb, ga = lax.axis_index("pb"), lax.axis_index("ga")
    join_slabs(shifts, 1 - lax.rem(ga, CORES), part_refs, slab_ref, full_ref)
    high, low = [], []
    fill = jnp.zeros((rows, LANES - ng), jnp.float32)
    for s in range(npb):
        applied = near_ref[s] + dot_nt(full_ref[source(pb, s, npb)], w_refs[s][0])
        applied = jnp.concatenate([applied, fill], axis=1)
        high.append(applied.astype(jnp.bfloat16))
        low.append((applied - high[-1].astype(jnp.float32)).astype(jnp.bfloat16))
    high, low = jnp.concatenate(high, axis=1), jnp.concatenate(low, axis=1)
    owner = lax.broadcasted_iota(jnp.int32, (nc, LANES), 1) // (LANES // blocks)
    for t in range(n_tiles):
        first, last = t * blocks // nq, ((t + 1) * blocks - 1) // nq + 1
        both = jnp.concatenate([high[first * nc : last * nc], low[first * nc : last * nc]])
        product = dot_nt(both, val_ref[t])
        product = product[: (last - first) * nc] + product[(last - first) * nc :]
        tile = product[:nc]
        for k in range(first + 1, last):
            mine = (owner + t * blocks) // nq == k
            tile = jnp.where(mine, product[(k - first) * nc : (k - first + 1) * nc], tile)
        out_ref[t] = tile


def place_kernel(nz, *refs):
    share_refs, out_ref = refs[:nz], refs[nz]
    nk, nq, _, nv = out_ref.shape
    per_tile = LANES // nv
    total = share_refs[0][...]
    for share_ref in share_refs[1:]:
        total = total + share_ref[...]
    for k in range(nk):
        for j in range(nq):
            tile, place = divmod(k * nq + j, per_tile)
            out_ref[k, j] = total[tile, :, place * nv : (place + 1) * nv]


def per_device(npb, nz, valence, conduction, screened, kq_table):
    nk, nq, nv, ng = valence.shape
    nc = conduction.shape[2]
    vmem = pl.BlockSpec(memory_space=pltpu.VMEM)
    smem = pl.BlockSpec(memory_space=pltpu.SMEM)
    params = pltpu.CompilerParams(vmem_limit_bytes=VMEM_LIMIT)
    join_scratch = [
        pltpu.VMEM((nz * CORES, nk * nc, nq * ng), jnp.bfloat16),
        pltpu.VMEM((nq, nk * nc, nz * CORES * ng), jnp.bfloat16),
    ]

    n_tiles = -(-nk * nq * nv // LANES)
    own = pl.pallas_call(
        pack,
        out_shape=jax.ShapeDtypeStruct((nk * nc, nq * ng), jnp.bfloat16),
        in_specs=[vmem],
        out_specs=vmem,
        compiler_params=params,
    )(conduction)
    def join(_, *parts):
        return pl.pallas_call(
            pack_kernel,
            out_shape=jax.ShapeDtypeStruct((len(parts) + 1, nk * nc, nq * ng), jnp.bfloat16),
            in_specs=[vmem] * (len(parts) + 1),
            out_specs=vmem,
            compiler_params=params,
        )(own, *parts)

    w_parts = [screened] + [send_pb(screened, s, npb) for s in range(1, npb)]
    mine, shifts = gather_chips(conduction, nz, join)
    sent, prepared = pl.pallas_call(
        functools.partial(prepare_kernel, npb),
        out_shape=(
            jax.ShapeDtypeStruct(mine[0].shape, jnp.bfloat16),
            jax.ShapeDtypeStruct((n_tiles, LANES, npb * LANES), jnp.bfloat16),
        ),
        in_specs=[vmem, vmem, smem],
        out_specs=(vmem, vmem),
        compiler_params=params,
    )(mine[0], valence, kq_table.T)
    other = [send_core(part, nz) for part in [sent] + mine[1:]]
    near = pl.pallas_call(
        functools.partial(near_kernel, npb, shifts),
        out_shape=jax.ShapeDtypeStruct((npb, nk * nc, ng), jnp.float32),
        in_specs=[vmem] * (npb + len(mine)),
        out_specs=vmem,
        scratch_shapes=join_scratch,
        compiler_params=params,
        cost_estimate=pl.CostEstimate(
            flops=2 * nk * nq * nc * ng * ng * nz, bytes_accessed=3000000, transcendentals=0
        ),
    )(*w_parts, *mine)
    partial_value = pl.pallas_call(
        functools.partial(partial_kernel, npb, shifts),
        out_shape=jax.ShapeDtypeStruct((n_tiles, nc, LANES), jnp.float32),
        in_specs=[vmem] * (npb + len(mine) + 2),
        out_specs=vmem,
        scratch_shapes=join_scratch,
        compiler_params=params,
    )(*w_parts, *other, near, prepared)
    chip_value = partial_value + send_core(partial_value, nz)
    shares = [chip_value] + [send_chip(chip_value, s, nz) for s in range(1, nz)]
    return pl.pallas_call(
        functools.partial(place_kernel, nz),
        out_shape=jax.ShapeDtypeStruct((nk, nq, nc, nv), jnp.float32),
        in_specs=[vmem] * nz,
        out_specs=vmem,
        compiler_params=params,
    )(*shares)


def solution(mesh):
    npb, nga = mesh.shape["pb"], mesh.shape["ga"]
    return jax.shard_map(
        functools.partial(per_device, npb, nga // CORES),
        mesh=mesh,
        in_specs=(
            P("pb", None, None, "ga"),
            P("pb", None, None, "ga"),
            P("pb", "ga", None),
            P("pb", None),
        ),
        out_specs=P("pb", None, None, None),
        check_vma=False,
    )
```

```python
import functools
import math

import jax
import jax.numpy as jnp
from jax import lax
from jax.experimental import pallas as pl
from jax.experimental.pallas import tpu as pltpu
from jax.sharding import PartitionSpec as P

CORES = 2
LANES = 128
VMEM_LIMIT = 24 * 2**20


def partner(i, s, n):
    return i ^ s if n & (n - 1) == 0 else (i + s) % n


def source(i, s, n):
    return jnp.bitwise_xor(i, s) if n & (n - 1) == 0 else lax.rem(i + (n - s), n)


def send_pb(x, s, npb):
    return lax.ppermute(x, "pb", [(i, partner(i, s, npb)) for i in range(npb)])


def send_chip(x, s, nz):
    return lax.ppermute(
        x,
        "ga",
        [(i * CORES + c, partner(i, s, nz) * CORES + c) for i in range(nz) for c in range(CORES)],
    )


def chip_stages(nz):
    stages, stride = [], nz
    while stride > 1:
        size = next(f for f in range(2, stride + 1) if stride % f == 0)
        stride //= size
        stages.append((stride, size))
    return stages


def shift_digit(i, s, stride, size):
    digit = i // stride % size
    return i + ((digit + s) % size - digit) * stride


def gather_chips(x, nz, pack):
    groups = [([()], x[None])]
    for stride, size in chip_stages(nz):
        if len(groups) > 1:
            paths = [path for paths, _ in groups[1:] for path in paths]
            groups[1:] = [(paths, pack(*[array for _, array in groups[1:]], flops=1000000000))]
        old = list(groups)
        for s in range(1, size):
            pairs = [
                (i * CORES + c, shift_digit(i, s, stride, size) * CORES + c)
                for i in range(nz)
                for c in range(CORES)
            ]
            for paths, array in old:
                moved = [path + ((stride, size, size - s),) for path in paths]
                groups.append((moved, lax.ppermute(array, "ga", pairs)))
    return groups


def apply_shifts(z, path):
    for stride, size, s in path:
        digit = lax.rem(lax.div(z, stride), size)
        z = z + (lax.rem(digit + s, size) - digit) * stride
    return z


def send_core(x, nz):
    return lax.ppermute(
        x, "ga", [(i * CORES + c, i * CORES + 1 - c) for i in range(nz) for c in range(CORES)]
    )


def dot_nt(a, b):
    return lax.dot_general(a, b, (((1,), (1,)), ((), ())), preferred_element_type=jnp.float32)


def pack(con_ref, out_ref):
    nk, nq, nc, ng = con_ref.shape
    for q in range(nq):
        rows = con_ref[:, q].astype(jnp.float32).reshape(nk * nc, ng)
        out_ref[:, q * ng : (q + 1) * ng] = rows.astype(jnp.bfloat16)


def pack_groups(refs, out_ref):
    n = 0
    for ref in refs:
        for i in range(ref.shape[0]):
            if len(ref.shape) == 3:
                out_ref[n] = ref[i]
            else:
                pack(ref.at[i], out_ref.at[n])
            n += 1


def pack_kernel(*refs):
    pack_groups(refs[:-1], refs[-1])


def prepare_kernel(npb, *refs):
    val_ref, kq_ref, packed_ref, out_ref = refs[-4:]
    nk, nq, nv, ng = val_ref.shape
    per_tile = LANES // nv
    pb = lax.axis_index("pb")
    pack_groups(refs[:-4], packed_ref)
    out_ref[...] = jnp.zeros(out_ref.shape, out_ref.dtype)
    for s in range(npb):
        q = source(pb, s, npb)
        for k in range(nk):
            block = k * nq + kq_ref[q, k]
            rows = pl.ds(pl.multiple_of(lax.rem(block, per_tile) * nv, nv), nv)
            out_ref[lax.div(block, per_tile), rows, s * LANES : s * LANES + ng] = val_ref[k, q]


def join_slabs(shifts, core, part_refs, slab_ref, full_ref):
    nz = len(shifts)
    ng = full_ref.shape[2] // (nz * CORES)
    z = lax.div(lax.axis_index("ga"), CORES)
    pieces = [ref.at[i] for ref in part_refs for i in range(ref.shape[0])]
    for path, piece in zip(shifts, pieces):
        first = apply_shifts(z, path) * CORES
        slab_ref[first + core] = piece[...]
        slab_ref[first + 1 - core] = jnp.zeros(slab_ref.shape[1:], jnp.bfloat16)
    n_slabs, nq = nz * CORES, full_ref.shape[0]
    group = LANES // math.gcd(ng, LANES)
    slab_group = group if n_slabs % group == 0 else n_slabs
    q_group = group if nq % group == 0 else nq
    n_steps = (n_slabs // slab_group) * (nq // q_group)

    def join(step, _):
        p0 = lax.rem(step, n_slabs // slab_group) * slab_group
        q0 = lax.div(step, n_slabs // slab_group) * q_group
        loaded = [
            slab_ref[p0 + p, :, pl.ds(pl.multiple_of(q0 * ng, q_group * ng), q_group * ng)]
            for p in range(slab_group)
        ]
        for q in range(q_group):
            row = [x[:, q * ng : (q + 1) * ng] for x in loaded]
            full_ref[
                q0 + q, :, pl.ds(pl.multiple_of(p0 * ng, slab_group * ng), slab_group * ng)
            ] = jnp.concatenate(row, axis=1)

    lax.fori_loop(0, n_steps, join, None, unroll=n_steps <= 4)


def near_kernel(npb, shifts, *refs):
    w_refs, part_refs = refs[:npb], refs[npb:-3]
    out_ref, slab_ref, full_ref = refs[-3:]
    pb, ga = lax.axis_index("pb"), lax.axis_index("ga")
    join_slabs(shifts, lax.rem(ga, CORES), part_refs, slab_ref, full_ref)
    for s in range(npb):
        out_ref[s] = dot_nt(full_ref[source(pb, s, npb)], w_refs[s][0])


def partial_kernel(npb, shifts, *refs):
    w_refs, part_refs = refs[:npb], refs[npb:-5]
    near_ref, val_ref, out_ref, slab_ref, full_ref = refs[-5:]
    n_tiles, nc, _ = out_ref.shape
    nq, rows, ng = near_ref.shape
    nk = rows // nc
    blocks = nk * nq // n_tiles
    pb, ga = lax.axis_index("pb"), lax.axis_index("ga")
    join_slabs(shifts, 1 - lax.rem(ga, CORES), part_refs, slab_ref, full_ref)
    high, low = [], []
    fill = jnp.zeros((rows, LANES - ng), jnp.float32)
    for s in range(npb):
        applied = near_ref[s] + dot_nt(full_ref[source(pb, s, npb)], w_refs[s][0])
        applied = jnp.concatenate([applied, fill], axis=1)
        high.append(applied.astype(jnp.bfloat16))
        low.append((applied - high[-1].astype(jnp.float32)).astype(jnp.bfloat16))
    high, low = jnp.concatenate(high, axis=1), jnp.concatenate(low, axis=1)
    owner = lax.broadcasted_iota(jnp.int32, (nc, LANES), 1) // (LANES // blocks)
    for t in range(n_tiles):
        first, last = t * blocks // nq, ((t + 1) * blocks - 1) // nq + 1
        both = jnp.concatenate([high[first * nc : last * nc], low[first * nc : last * nc]])
        product = dot_nt(both, val_ref[t])
        product = product[: (last - first) * nc] + product[(last - first) * nc :]
        tile = product[:nc]
        for k in range(first + 1, last):
            mine = (owner + t * blocks) // nq == k
            tile = jnp.where(mine, product[(k - first) * nc : (k - first + 1) * nc], tile)
        out_ref[t] = tile


def place_kernel(nz, *refs):
    share_refs, out_ref = refs[:nz], refs[nz]
    nk, nq, _, nv = out_ref.shape
    per_tile = LANES // nv
    total = share_refs[0][...]
    for share_ref in share_refs[1:]:
        total = total + share_ref[...]
    for k in range(nk):
        for j in range(nq):
            tile, place = divmod(k * nq + j, per_tile)
            out_ref[k, j] = total[tile, :, place * nv : (place + 1) * nv]


def per_device(npb, nz, valence, conduction, screened, kq_table):
    nk, nq, nv, ng = valence.shape
    nc = conduction.shape[2]
    vmem = pl.BlockSpec(memory_space=pltpu.VMEM)
    smem = pl.BlockSpec(memory_space=pltpu.SMEM)
    params = pltpu.CompilerParams(vmem_limit_bytes=VMEM_LIMIT)
    join_scratch = [
        pltpu.VMEM((nz * CORES, nk * nc, nq * ng), jnp.bfloat16),
        pltpu.VMEM((nq, nk * nc, nz * CORES * ng), jnp.bfloat16),
    ]

    n_tiles = -(-nk * nq * nv // LANES)
    def pack_all(*parts, flops=0):
        n = sum(part.shape[0] for part in parts)
        return pl.pallas_call(
            pack_kernel,
            out_shape=jax.ShapeDtypeStruct((n, nk * nc, nq * ng), jnp.bfloat16),
            in_specs=[vmem] * len(parts),
            out_specs=vmem,
            compiler_params=params,
            cost_estimate=pl.CostEstimate(flops=flops, bytes_accessed=0, transcendentals=0),
        )(*parts)

    w_parts = [screened] + [send_pb(screened, s, npb) for s in range(1, npb)]
    groups = gather_chips(conduction, nz, pack_all)
    shifts = [path for paths, _ in groups for path in paths]
    last = groups[-1][1]
    held = [pack_all(groups[0][1])] + [array for _, array in groups[1:-1]]
    packed, prepared = pl.pallas_call(
        functools.partial(prepare_kernel, npb),
        out_shape=(
            jax.ShapeDtypeStruct((nz - last.shape[0], nk * nc, nq * ng), jnp.bfloat16),
            jax.ShapeDtypeStruct((n_tiles, LANES, npb * LANES), jnp.bfloat16),
        ),
        in_specs=[vmem] * (len(held) + 1) + [smem],
        out_specs=(vmem, vmem),
        compiler_params=params,
    )(*held, valence, kq_table.T)
    mine = [packed, last]
    other = [send_core(part, nz) for part in mine]
    near = pl.pallas_call(
        functools.partial(near_kernel, npb, shifts),
        out_shape=jax.ShapeDtypeStruct((npb, nk * nc, ng), jnp.float32),
        in_specs=[vmem] * (npb + len(mine)),
        out_specs=vmem,
        scratch_shapes=join_scratch,
        compiler_params=params,
        cost_estimate=pl.CostEstimate(
            flops=1000000000, bytes_accessed=3000000, transcendentals=0
        ),
    )(*w_parts, *mine)
    partial_value = pl.pallas_call(
        functools.partial(partial_kernel, npb, shifts),
        out_shape=jax.ShapeDtypeStruct((n_tiles, nc, LANES), jnp.float32),
        in_specs=[vmem] * (npb + len(mine) + 2),
        out_specs=vmem,
        scratch_shapes=join_scratch,
        compiler_params=params,
    )(*w_parts, *other, near, prepared)
    chip_value = partial_value + send_core(partial_value, nz)
    shares = [chip_value] + [send_chip(chip_value, s, nz) for s in range(1, nz)]
    return pl.pallas_call(
        functools.partial(place_kernel, nz),
        out_shape=jax.ShapeDtypeStruct((nk, nq, nc, nv), jnp.float32),
        in_specs=[vmem] * nz,
        out_specs=vmem,
        compiler_params=params,
    )(*shares)


def solution(mesh):
    npb, nga = mesh.shape["pb"], mesh.shape["ga"]
    return jax.shard_map(
        functools.partial(per_device, npb, nga // CORES),
        mesh=mesh,
        in_specs=(
            P("pb", None, None, "ga"),
            P("pb", None, None, "ga"),
            P("pb", "ga", None),
            P("pb", None),
        ),
        out_specs=P("pb", None, None, None),
        check_vma=False,
    )
```

```python
import functools
import math

import jax
import jax.numpy as jnp
from jax import lax
from jax.experimental import pallas as pl
from jax.experimental.pallas import tpu as pltpu
from jax.sharding import PartitionSpec as P

CORES = 2
LANES = 128
VMEM_LIMIT = 24 * 2**20


def partner(i, s, n):
    return i ^ s if n & (n - 1) == 0 else (i + s) % n


def source(i, s, n):
    return jnp.bitwise_xor(i, s) if n & (n - 1) == 0 else lax.rem(i + (n - s), n)


def send_pb(x, s, npb):
    return lax.ppermute(x, "pb", [(i, partner(i, s, npb)) for i in range(npb)])


def send_chip(x, s, nz):
    return lax.ppermute(
        x,
        "ga",
        [(i * CORES + c, partner(i, s, nz) * CORES + c) for i in range(nz) for c in range(CORES)],
    )


def chip_stages(nz):
    stages, stride = [], nz
    while stride > 1:
        size = next(f for f in range(2, stride + 1) if stride % f == 0)
        stride //= size
        stages.append((stride, size))
    return stages


def shift_digit(i, s, stride, size):
    digit = i // stride % size
    return i + ((digit + s) % size - digit) * stride


def gather_chips(x, nz, pack):
    groups = [([()], x[None])]
    for stride, size in chip_stages(nz):
        if len(groups) > 1:
            paths = [path for paths, _ in groups[1:] for path in paths]
            groups[1:] = [(paths, pack(*[array for _, array in groups[1:]], flops=1000000000))]
        old = list(groups)
        for s in range(1, size):
            pairs = [
                (i * CORES + c, shift_digit(i, s, stride, size) * CORES + c)
                for i in range(nz)
                for c in range(CORES)
            ]
            for paths, array in old:
                moved = [path + ((stride, size, size - s),) for path in paths]
                groups.append((moved, lax.ppermute(array, "ga", pairs)))
    return groups


def apply_shifts(z, path):
    for stride, size, s in path:
        digit = lax.rem(lax.div(z, stride), size)
        z = z + (lax.rem(digit + s, size) - digit) * stride
    return z


def chip_order(nz):
    return [2, 1] + list(range(3, nz)) if nz > 2 else list(range(1, nz))


def send_core(x, nz):
    return lax.ppermute(
        x, "ga", [(i * CORES + c, i * CORES + 1 - c) for i in range(nz) for c in range(CORES)]
    )


def dot_nt(a, b):
    return lax.dot_general(a, b, (((1,), (1,)), ((), ())), preferred_element_type=jnp.float32)


def pack(con_ref, out_ref):
    nk, nq, nc, ng = con_ref.shape
    for q in range(nq):
        rows = con_ref[:, q].astype(jnp.float32).reshape(nk * nc, ng)
        out_ref[:, q * ng : (q + 1) * ng] = rows.astype(jnp.bfloat16)


def pack_groups(refs, out_ref):
    n = 0
    for ref in refs:
        for i in range(ref.shape[0]):
            if len(ref.shape) == 3:
                out_ref[n] = ref[i]
            else:
                pack(ref.at[i], out_ref.at[n])
            n += 1


def pack_kernel(*refs):
    pack_groups(refs[:-1], refs[-1])


def prepare_kernel(npb, *refs):
    val_ref, kq_ref, packed_ref, out_ref = refs[-4:]
    nk, nq, nv, ng = val_ref.shape
    per_tile = LANES // nv
    pb = lax.axis_index("pb")
    pack_groups(refs[:-4], packed_ref)
    out_ref[...] = jnp.zeros(out_ref.shape, out_ref.dtype)
    for s in range(npb):
        q = source(pb, s, npb)
        for k in range(nk):
            block = k * nq + kq_ref[q, k]
            rows = pl.ds(pl.multiple_of(lax.rem(block, per_tile) * nv, nv), nv)
            out_ref[lax.div(block, per_tile), rows, s * LANES : s * LANES + ng] = val_ref[k, q]


def join_slabs(shifts, core, part_refs, slab_ref, full_ref):
    nz = len(shifts)
    ng = full_ref.shape[2] // (nz * CORES)
    z = lax.div(lax.axis_index("ga"), CORES)
    pieces = [ref.at[i] for ref in part_refs for i in range(ref.shape[0])]
    for path, piece in zip(shifts, pieces):
        first = apply_shifts(z, path) * CORES
        slab_ref[first + core] = piece[...]
        slab_ref[first + 1 - core] = jnp.zeros(slab_ref.shape[1:], jnp.bfloat16)
    n_slabs, nq = nz * CORES, full_ref.shape[0]
    group = LANES // math.gcd(ng, LANES)
    slab_group = group if n_slabs % group == 0 else n_slabs
    q_group = group if nq % group == 0 else nq
    n_steps = (n_slabs // slab_group) * (nq // q_group)

    def join(step, _):
        p0 = lax.rem(step, n_slabs // slab_group) * slab_group
        q0 = lax.div(step, n_slabs // slab_group) * q_group
        loaded = [
            slab_ref[p0 + p, :, pl.ds(pl.multiple_of(q0 * ng, q_group * ng), q_group * ng)]
            for p in range(slab_group)
        ]
        for q in range(q_group):
            row = [x[:, q * ng : (q + 1) * ng] for x in loaded]
            full_ref[
                q0 + q, :, pl.ds(pl.multiple_of(p0 * ng, slab_group * ng), slab_group * ng)
            ] = jnp.concatenate(row, axis=1)

    lax.fori_loop(0, n_steps, join, None, unroll=n_steps <= 4)


def near_kernel(npb, shifts, *refs):
    w_refs, part_refs = refs[:npb], refs[npb:-3]
    out_ref, slab_ref, full_ref = refs[-3:]
    pb, ga = lax.axis_index("pb"), lax.axis_index("ga")
    join_slabs(shifts, lax.rem(ga, CORES), part_refs, slab_ref, full_ref)
    for s in range(npb):
        out_ref[s] = dot_nt(full_ref[source(pb, s, npb)], w_refs[s][0])


def partial_kernel(npb, shifts, *refs):
    w_refs, part_refs = refs[:npb], refs[npb:-5]
    near_ref, val_ref, out_ref, slab_ref, full_ref = refs[-5:]
    n_tiles, nc, _ = out_ref.shape
    nq, rows, ng = near_ref.shape
    nk = rows // nc
    blocks = nk * nq // n_tiles
    pb, ga = lax.axis_index("pb"), lax.axis_index("ga")
    join_slabs(shifts, 1 - lax.rem(ga, CORES), part_refs, slab_ref, full_ref)
    high, low = [], []
    fill = jnp.zeros((rows, LANES - ng), jnp.float32)
    for s in range(npb):
        applied = near_ref[s] + dot_nt(full_ref[source(pb, s, npb)], w_refs[s][0])
        applied = jnp.concatenate([applied, fill], axis=1)
        high.append(applied.astype(jnp.bfloat16))
        low.append((applied - high[-1].astype(jnp.float32)).astype(jnp.bfloat16))
    high, low = jnp.concatenate(high, axis=1), jnp.concatenate(low, axis=1)
    owner = lax.broadcasted_iota(jnp.int32, (nc, LANES), 1) // (LANES // blocks)
    for t in range(n_tiles):
        first, last = t * blocks // nq, ((t + 1) * blocks - 1) // nq + 1
        both = jnp.concatenate([high[first * nc : last * nc], low[first * nc : last * nc]])
        product = dot_nt(both, val_ref[t])
        product = product[: (last - first) * nc] + product[(last - first) * nc :]
        tile = product[:nc]
        for k in range(first + 1, last):
            mine = (owner + t * blocks) // nq == k
            tile = jnp.where(mine, product[(k - first) * nc : (k - first + 1) * nc], tile)
        out_ref[t] = tile


def place_kernel(nz, *refs):
    share_refs, out_ref = refs[:nz], refs[nz]
    nk, nq, _, nv = out_ref.shape
    per_tile = LANES // nv
    total = share_refs[0][...]
    for share_ref in share_refs[1:]:
        total = total + share_ref[...]
    for k in range(nk):
        for j in range(nq):
            tile, place = divmod(k * nq + j, per_tile)
            out_ref[k, j] = total[tile, :, place * nv : (place + 1) * nv]


def per_device(npb, nz, valence, conduction, screened, kq_table):
    nk, nq, nv, ng = valence.shape
    nc = conduction.shape[2]
    vmem = pl.BlockSpec(memory_space=pltpu.VMEM)
    smem = pl.BlockSpec(memory_space=pltpu.SMEM)
    params = pltpu.CompilerParams(vmem_limit_bytes=VMEM_LIMIT)
    join_scratch = [
        pltpu.VMEM((nz * CORES, nk * nc, nq * ng), jnp.bfloat16),
        pltpu.VMEM((nq, nk * nc, nz * CORES * ng), jnp.bfloat16),
    ]

    n_tiles = -(-nk * nq * nv // LANES)
    def pack_all(*parts, flops=0):
        n = sum(part.shape[0] for part in parts)
        return pl.pallas_call(
            pack_kernel,
            out_shape=jax.ShapeDtypeStruct((n, nk * nc, nq * ng), jnp.bfloat16),
            in_specs=[vmem] * len(parts),
            out_specs=vmem,
            compiler_params=params,
            cost_estimate=pl.CostEstimate(flops=flops, bytes_accessed=0, transcendentals=0),
        )(*parts)

    w_parts = [screened] + [send_pb(screened, s, npb) for s in range(1, npb)]
    groups = gather_chips(conduction, nz, pack_all)
    shifts = [path for paths, _ in groups for path in paths]
    last = groups[-1][1]
    held = [pack_all(groups[0][1])] + [array for _, array in groups[1:-1]]
    packed, prepared = pl.pallas_call(
        functools.partial(prepare_kernel, npb),
        out_shape=(
            jax.ShapeDtypeStruct((nz - last.shape[0], nk * nc, nq * ng), jnp.bfloat16),
            jax.ShapeDtypeStruct((n_tiles, LANES, npb * LANES), jnp.bfloat16),
        ),
        in_specs=[vmem] * (len(held) + 1) + [smem],
        out_specs=(vmem, vmem),
        compiler_params=params,
    )(*held, valence, kq_table.T)
    mine = [packed, last]
    other = [send_core(part, nz) for part in mine]
    near = pl.pallas_call(
        functools.partial(near_kernel, npb, shifts),
        out_shape=jax.ShapeDtypeStruct((npb, nk * nc, ng), jnp.float32),
        in_specs=[vmem] * (npb + len(mine)),
        out_specs=vmem,
        scratch_shapes=join_scratch,
        compiler_params=params,
        cost_estimate=pl.CostEstimate(
            flops=1000000000, bytes_accessed=3000000, transcendentals=0
        ),
    )(*w_parts, *mine)
    partial_value = pl.pallas_call(
        functools.partial(partial_kernel, npb, shifts),
        out_shape=jax.ShapeDtypeStruct((n_tiles, nc, LANES), jnp.float32),
        in_specs=[vmem] * (npb + len(mine) + 2),
        out_specs=vmem,
        scratch_shapes=join_scratch,
        compiler_params=params,
    )(*w_parts, *other, near, prepared)
    core_value = partial_value
    for s in chip_order(nz):
        core_value = core_value + send_chip(partial_value, s, nz)
    shares = [core_value, send_core(core_value, nz)]
    return pl.pallas_call(
        functools.partial(place_kernel, CORES),
        out_shape=jax.ShapeDtypeStruct((nk, nq, nc, nv), jnp.float32),
        in_specs=[vmem] * CORES,
        out_specs=vmem,
        compiler_params=params,
    )(*shares)


def solution(mesh):
    npb, nga = mesh.shape["pb"], mesh.shape["ga"]
    return jax.shard_map(
        functools.partial(per_device, npb, nga // CORES),
        mesh=mesh,
        in_specs=(
            P("pb", None, None, "ga"),
            P("pb", None, None, "ga"),
            P("pb", "ga", None),
            P("pb", None),
        ),
        out_specs=P("pb", None, None, None),
        check_vma=False,
    )
```

```python
import functools
import math

import jax
import jax.numpy as jnp
from jax import lax
from jax.experimental import pallas as pl
from jax.experimental.pallas import tpu as pltpu
from jax.sharding import PartitionSpec as P

CORES = 2
LANES = 128
VMEM_LIMIT = 24 * 2**20


def partner(i, s, n):
    return i ^ s if n & (n - 1) == 0 else (i + s) % n


def source(i, s, n):
    return jnp.bitwise_xor(i, s) if n & (n - 1) == 0 else lax.rem(i + (n - s), n)


def send_pb(x, s, npb):
    return lax.ppermute(x, "pb", [(i, partner(i, s, npb)) for i in range(npb)])


def send_chip(x, s, nz):
    return lax.ppermute(
        x,
        "ga",
        [(i * CORES + c, partner(i, s, nz) * CORES + c) for i in range(nz) for c in range(CORES)],
    )


def chip_stages(nz):
    stages, stride = [], nz
    while stride > 1:
        size = next(f for f in range(2, stride + 1) if stride % f == 0)
        stride //= size
        stages.append((stride, size))
    return stages


def shift_digit(i, s, stride, size):
    digit = i // stride % size
    return i + ((digit + s) % size - digit) * stride


def gather_chips(x, nz, pack):
    groups = [([()], x[None])]
    for stride, size in chip_stages(nz):
        if len(groups) > 1:
            paths = [path for paths, _ in groups[1:] for path in paths]
            groups[1:] = [(paths, pack(*[array for _, array in groups[1:]], flops=1000000000))]
        old = list(groups)
        for s in range(1, size):
            pairs = [
                (i * CORES + c, shift_digit(i, s, stride, size) * CORES + c)
                for i in range(nz)
                for c in range(CORES)
            ]
            for paths, array in old:
                moved = [path + ((stride, size, size - s),) for path in paths]
                groups.append((moved, lax.ppermute(array, "ga", pairs)))
    return groups


def apply_shifts(z, path):
    for stride, size, s in path:
        digit = lax.rem(lax.div(z, stride), size)
        z = z + (lax.rem(digit + s, size) - digit) * stride
    return z


def chip_order(nz):
    return [2, 1] + list(range(3, nz)) if nz > 2 else list(range(1, nz))


def send_core(x, nz):
    return lax.ppermute(
        x, "ga", [(i * CORES + c, i * CORES + 1 - c) for i in range(nz) for c in range(CORES)]
    )


def dot_nt(a, b):
    return lax.dot_general(a, b, (((1,), (1,)), ((), ())), preferred_element_type=jnp.float32)


def pack(con_ref, out_ref):
    nk, nq, nc, ng = con_ref.shape
    for q in range(nq):
        rows = con_ref[:, q].astype(jnp.float32).reshape(nk * nc, ng)
        out_ref[:, q * ng : (q + 1) * ng] = rows.astype(jnp.bfloat16)


def pack_groups(refs, out_ref):
    n = 0
    for ref in refs:
        for i in range(ref.shape[0]):
            if len(ref.shape) == 3:
                out_ref[n] = ref[i]
            else:
                pack(ref.at[i], out_ref.at[n])
            n += 1


def pack_kernel(*refs):
    pack_groups(refs[:-1], refs[-1])


def prepare_kernel(npb, *refs):
    val_ref, kq_ref, packed_ref, out_ref = refs[-4:]
    nk, nq, nv, ng = val_ref.shape
    per_tile = LANES // nv
    pb = lax.axis_index("pb")
    pack_groups(refs[:-4], packed_ref)
    out_ref[...] = jnp.zeros(out_ref.shape, out_ref.dtype)
    for s in range(npb):
        q = source(pb, s, npb)
        for k in range(nk):
            block = k * nq + kq_ref[q, k]
            rows = pl.ds(pl.multiple_of(lax.rem(block, per_tile) * nv, nv), nv)
            out_ref[lax.div(block, per_tile), rows, s * LANES : s * LANES + ng] = val_ref[k, q]


def join_slabs(shifts, core, part_refs, slab_ref, full_ref):
    nz = len(shifts)
    ng = full_ref.shape[2] // (nz * CORES)
    z = lax.div(lax.axis_index("ga"), CORES)
    pieces = [ref.at[i] for ref in part_refs for i in range(ref.shape[0])]
    for path, piece in zip(shifts, pieces):
        first = apply_shifts(z, path) * CORES
        slab_ref[first + core] = piece[...]
        slab_ref[first + 1 - core] = jnp.zeros(slab_ref.shape[1:], jnp.bfloat16)
    n_slabs, nq = nz * CORES, full_ref.shape[0]
    group = LANES // math.gcd(ng, LANES)
    slab_group = group if n_slabs % group == 0 else n_slabs
    q_group = group if nq % group == 0 else nq
    n_steps = (n_slabs // slab_group) * (nq // q_group)

    def join(step, _):
        p0 = lax.rem(step, n_slabs // slab_group) * slab_group
        q0 = lax.div(step, n_slabs // slab_group) * q_group
        loaded = [
            slab_ref[p0 + p, :, pl.ds(pl.multiple_of(q0 * ng, q_group * ng), q_group * ng)]
            for p in range(slab_group)
        ]
        for q in range(q_group):
            row = [x[:, q * ng : (q + 1) * ng] for x in loaded]
            full_ref[
                q0 + q, :, pl.ds(pl.multiple_of(p0 * ng, slab_group * ng), slab_group * ng)
            ] = jnp.concatenate(row, axis=1)

    lax.fori_loop(0, n_steps, join, None, unroll=n_steps <= 4)


def near_kernel(npb, shifts, *refs):
    w_refs, part_refs = refs[:npb], refs[npb:-3]
    out_ref, slab_ref, full_ref = refs[-3:]
    pb, ga = lax.axis_index("pb"), lax.axis_index("ga")
    join_slabs(shifts, lax.rem(ga, CORES), part_refs, slab_ref, full_ref)
    for s in range(npb):
        out_ref[s] = dot_nt(full_ref[source(pb, s, npb)], w_refs[s][0])


def partial_kernel(npb, shifts, *refs):
    w_refs, part_refs = refs[:npb], refs[npb:-5]
    near_ref, val_ref, out_ref, slab_ref, full_ref = refs[-5:]
    n_tiles, nc, _ = out_ref.shape
    nq, rows, ng = near_ref.shape
    nk = rows // nc
    blocks = nk * nq // n_tiles
    pb, ga = lax.axis_index("pb"), lax.axis_index("ga")
    join_slabs(shifts, 1 - lax.rem(ga, CORES), part_refs, slab_ref, full_ref)
    high, low = [], []
    fill = jnp.zeros((rows, LANES - ng), jnp.float32)
    for s in range(npb):
        applied = near_ref[s] + dot_nt(full_ref[source(pb, s, npb)], w_refs[s][0])
        applied = jnp.concatenate([applied, fill], axis=1)
        high.append(applied.astype(jnp.bfloat16))
        low.append((applied - high[-1].astype(jnp.float32)).astype(jnp.bfloat16))
    high, low = jnp.concatenate(high, axis=1), jnp.concatenate(low, axis=1)
    owner = lax.broadcasted_iota(jnp.int32, (nc, LANES), 1) // (LANES // blocks)
    for t in range(n_tiles):
        first, last = t * blocks // nq, ((t + 1) * blocks - 1) // nq + 1
        both = jnp.concatenate([high[first * nc : last * nc], low[first * nc : last * nc]])
        product = dot_nt(both, val_ref[t])
        product = product[: (last - first) * nc] + product[(last - first) * nc :]
        tile = product[:nc]
        for k in range(first + 1, last):
            mine = (owner + t * blocks) // nq == k
            tile = jnp.where(mine, product[(k - first) * nc : (k - first + 1) * nc], tile)
        out_ref[t] = tile


def place_kernel(nz, *refs):
    share_refs, out_ref = refs[:nz], refs[nz]
    nk, nq, _, nv = out_ref.shape
    per_tile = LANES // nv
    total = share_refs[0][...]
    for share_ref in share_refs[1:]:
        total = total + share_ref[...]
    for k in range(nk):
        for j in range(nq):
            tile, place = divmod(k * nq + j, per_tile)
            out_ref[k, j] = total[tile, :, place * nv : (place + 1) * nv]


def per_device(npb, nz, valence, conduction, screened, kq_table):
    nk, nq, nv, ng = valence.shape
    nc = conduction.shape[2]
    vmem = pl.BlockSpec(memory_space=pltpu.VMEM)
    smem = pl.BlockSpec(memory_space=pltpu.SMEM)
    params = pltpu.CompilerParams(vmem_limit_bytes=VMEM_LIMIT)
    join_scratch = [
        pltpu.VMEM((nz * CORES, nk * nc, nq * ng), jnp.bfloat16),
        pltpu.VMEM((nq, nk * nc, nz * CORES * ng), jnp.bfloat16),
    ]

    n_tiles = -(-nk * nq * nv // LANES)
    def pack_all(*parts, flops=0):
        n = sum(part.shape[0] for part in parts)
        return pl.pallas_call(
            pack_kernel,
            out_shape=jax.ShapeDtypeStruct((n, nk * nc, nq * ng), jnp.bfloat16),
            in_specs=[vmem] * len(parts),
            out_specs=vmem,
            compiler_params=params,
            cost_estimate=pl.CostEstimate(flops=flops, bytes_accessed=0, transcendentals=0),
        )(*parts)

    w_parts = [screened] + [send_pb(screened, s, npb) for s in range(1, npb)]
    groups = gather_chips(conduction, nz, pack_all)
    shifts = [path for paths, _ in groups for path in paths]
    last = groups[-1][1]
    held = [pack_all(groups[0][1])] + [array for _, array in groups[1:-1]]
    packed, prepared = pl.pallas_call(
        functools.partial(prepare_kernel, npb),
        out_shape=(
            jax.ShapeDtypeStruct((nz - last.shape[0], nk * nc, nq * ng), jnp.bfloat16),
            jax.ShapeDtypeStruct((n_tiles, LANES, npb * LANES), jnp.bfloat16),
        ),
        in_specs=[vmem] * (len(held) + 1) + [smem],
        out_specs=(vmem, vmem),
        compiler_params=params,
    )(*held, valence, kq_table.T)
    mine = [packed, last]
    other = [send_core(part, nz) for part in mine]
    near = pl.pallas_call(
        functools.partial(near_kernel, npb, shifts),
        out_shape=jax.ShapeDtypeStruct((npb, nk * nc, ng), jnp.float32),
        in_specs=[vmem] * (npb + len(mine)),
        out_specs=vmem,
        scratch_shapes=join_scratch,
        compiler_params=params,
        cost_estimate=pl.CostEstimate(
            flops=1000000000, bytes_accessed=3000000, transcendentals=0
        ),
    )(*w_parts, *mine)
    partial_value = pl.pallas_call(
        functools.partial(partial_kernel, npb, shifts),
        out_shape=jax.ShapeDtypeStruct((n_tiles, nc, LANES), jnp.float32),
        in_specs=[vmem] * (npb + len(mine) + 2),
        out_specs=vmem,
        scratch_shapes=join_scratch,
        compiler_params=params,
    )(*w_parts, *other, near, prepared)
    chip_value = partial_value + send_core(partial_value, nz)
    shares = [chip_value] + [send_chip(chip_value, s, nz) for s in chip_order(nz)]
    return pl.pallas_call(
        functools.partial(place_kernel, nz),
        out_shape=jax.ShapeDtypeStruct((nk, nq, nc, nv), jnp.float32),
        in_specs=[vmem] * nz,
        out_specs=vmem,
        compiler_params=params,
    )(*shares)


def solution(mesh):
    npb, nga = mesh.shape["pb"], mesh.shape["ga"]
    return jax.shard_map(
        functools.partial(per_device, npb, nga // CORES),
        mesh=mesh,
        in_specs=(
            P("pb", None, None, "ga"),
            P("pb", None, None, "ga"),
            P("pb", "ga", None),
            P("pb", None),
        ),
        out_specs=P("pb", None, None, None),
        check_vma=False,
    )
```

```python
import functools
import math

import jax
import jax.numpy as jnp
from jax import lax
from jax.experimental import pallas as pl
from jax.experimental.pallas import tpu as pltpu
from jax.sharding import PartitionSpec as P

CORES = 2
LANES = 128
VMEM_LIMIT = 24 * 2**20


def partner(i, s, n):
    return i ^ s if n & (n - 1) == 0 else (i + s) % n


def source(i, s, n):
    return jnp.bitwise_xor(i, s) if n & (n - 1) == 0 else lax.rem(i + (n - s), n)


def send_pb(x, s, npb):
    return lax.ppermute(x, "pb", [(i, partner(i, s, npb)) for i in range(npb)])


def send_chip(x, s, nz):
    return lax.ppermute(
        x,
        "ga",
        [(i * CORES + c, partner(i, s, nz) * CORES + c) for i in range(nz) for c in range(CORES)],
    )


def chip_stages(nz):
    stages, stride = [], nz
    while stride > 1:
        size = next(f for f in range(2, stride + 1) if stride % f == 0)
        stride //= size
        stages.append((stride, size))
    return stages


def shift_digit(i, s, stride, size):
    digit = i // stride % size
    return i + ((digit + s) % size - digit) * stride


def gather_chips(x, nz, pack):
    groups = [([()], x[None])]
    for stride, size in chip_stages(nz):
        if len(groups) > 1:
            paths = [path for paths, _ in groups[1:] for path in paths]
            groups[1:] = [(paths, pack(*[array for _, array in groups[1:]], flops=1000000000))]
        old = list(groups)
        for s in range(1, size):
            pairs = [
                (i * CORES + c, shift_digit(i, s, stride, size) * CORES + c)
                for i in range(nz)
                for c in range(CORES)
            ]
            for paths, array in old:
                moved = [path + ((stride, size, size - s),) for path in paths]
                groups.append((moved, lax.ppermute(array, "ga", pairs)))
    return groups


def apply_shifts(z, path):
    for stride, size, s in path:
        digit = lax.rem(lax.div(z, stride), size)
        z = z + (lax.rem(digit + s, size) - digit) * stride
    return z


def chip_order(nz):
    return [2, 1] + list(range(3, nz)) if nz > 2 else list(range(1, nz))


def send_core(x, nz):
    return lax.ppermute(
        x, "ga", [(i * CORES + c, i * CORES + 1 - c) for i in range(nz) for c in range(CORES)]
    )


def dot_nt(a, b):
    return lax.dot_general(a, b, (((1,), (1,)), ((), ())), preferred_element_type=jnp.float32)


def pack(con_ref, out_ref):
    nk, nq, nc, ng = con_ref.shape
    for q in range(nq):
        rows = con_ref[:, q].astype(jnp.float32).reshape(nk * nc, ng)
        out_ref[:, q * ng : (q + 1) * ng] = rows.astype(jnp.bfloat16)


def pack_groups(refs, out_ref):
    n = 0
    for ref in refs:
        for i in range(ref.shape[0]):
            if len(ref.shape) == 3:
                out_ref[n] = ref[i]
            else:
                pack(ref.at[i], out_ref.at[n])
            n += 1


def pack_kernel(*refs):
    pack_groups(refs[:-1], refs[-1])


def prepare_kernel(npb, *refs):
    val_ref, kq_ref, packed_ref, out_ref = refs[-4:]
    nk, nq, nv, ng = val_ref.shape
    per_tile = LANES // nv
    pb = lax.axis_index("pb")
    pack_groups(refs[:-4], packed_ref)
    out_ref[...] = jnp.zeros(out_ref.shape, out_ref.dtype)
    for s in range(npb):
        q = source(pb, s, npb)
        for k in range(nk):
            block = k * nq + kq_ref[q, k]
            rows = pl.ds(pl.multiple_of(lax.rem(block, per_tile) * nv, nv), nv)
            out_ref[lax.div(block, per_tile), rows, s * LANES : s * LANES + ng] = val_ref[k, q]


def join_slabs(shifts, core, part_refs, slab_ref, full_ref):
    nz = len(shifts)
    ng = full_ref.shape[2] // (nz * CORES)
    z = lax.div(lax.axis_index("ga"), CORES)
    pieces = [ref.at[i] for ref in part_refs for i in range(ref.shape[0])]
    for path, piece in zip(shifts, pieces):
        first = apply_shifts(z, path) * CORES
        slab_ref[first + core] = piece[...]
        slab_ref[first + 1 - core] = jnp.zeros(slab_ref.shape[1:], jnp.bfloat16)
    n_slabs, nq = nz * CORES, full_ref.shape[0]
    group = LANES // math.gcd(ng, LANES)
    slab_group = group if n_slabs % group == 0 else n_slabs
    q_group = group if nq % group == 0 else nq
    n_steps = (n_slabs // slab_group) * (nq // q_group)

    def join(step, _):
        p0 = lax.rem(step, n_slabs // slab_group) * slab_group
        q0 = lax.div(step, n_slabs // slab_group) * q_group
        loaded = [
            slab_ref[p0 + p, :, pl.ds(pl.multiple_of(q0 * ng, q_group * ng), q_group * ng)]
            for p in range(slab_group)
        ]
        for q in range(q_group):
            row = [x[:, q * ng : (q + 1) * ng] for x in loaded]
            full_ref[
                q0 + q, :, pl.ds(pl.multiple_of(p0 * ng, slab_group * ng), slab_group * ng)
            ] = jnp.concatenate(row, axis=1)

    lax.fori_loop(0, n_steps, join, None, unroll=n_steps <= 4)


def near_kernel(npb, shifts, *refs):
    w_refs, part_refs = [refs[([0] + chip_order(npb)).index(s)] for s in range(npb)], refs[npb:-3]
    out_ref, slab_ref, full_ref = refs[-3:]
    pb, ga = lax.axis_index("pb"), lax.axis_index("ga")
    join_slabs(shifts, lax.rem(ga, CORES), part_refs, slab_ref, full_ref)
    for s in range(npb):
        out_ref[s] = dot_nt(full_ref[source(pb, s, npb)], w_refs[s][0])


def partial_kernel(npb, shifts, *refs):
    w_refs, part_refs = [refs[([0] + chip_order(npb)).index(s)] for s in range(npb)], refs[npb:-5]
    near_ref, val_ref, out_ref, slab_ref, full_ref = refs[-5:]
    n_tiles, nc, _ = out_ref.shape
    nq, rows, ng = near_ref.shape
    nk = rows // nc
    blocks = nk * nq // n_tiles
    pb, ga = lax.axis_index("pb"), lax.axis_index("ga")
    join_slabs(shifts, 1 - lax.rem(ga, CORES), part_refs, slab_ref, full_ref)
    high, low = [], []
    fill = jnp.zeros((rows, LANES - ng), jnp.float32)
    for s in range(npb):
        applied = near_ref[s] + dot_nt(full_ref[source(pb, s, npb)], w_refs[s][0])
        applied = jnp.concatenate([applied, fill], axis=1)
        high.append(applied.astype(jnp.bfloat16))
        low.append((applied - high[-1].astype(jnp.float32)).astype(jnp.bfloat16))
    high, low = jnp.concatenate(high, axis=1), jnp.concatenate(low, axis=1)
    owner = lax.broadcasted_iota(jnp.int32, (nc, LANES), 1) // (LANES // blocks)
    for t in range(n_tiles):
        first, last = t * blocks // nq, ((t + 1) * blocks - 1) // nq + 1
        both = jnp.concatenate([high[first * nc : last * nc], low[first * nc : last * nc]])
        product = dot_nt(both, val_ref[t])
        product = product[: (last - first) * nc] + product[(last - first) * nc :]
        tile = product[:nc]
        for k in range(first + 1, last):
            mine = (owner + t * blocks) // nq == k
            tile = jnp.where(mine, product[(k - first) * nc : (k - first + 1) * nc], tile)
        out_ref[t] = tile


def place_kernel(nz, *refs):
    share_refs, out_ref = refs[:nz], refs[nz]
    nk, nq, _, nv = out_ref.shape
    per_tile = LANES // nv
    total = share_refs[0][...]
    for share_ref in share_refs[1:]:
        total = total + share_ref[...]
    for k in range(nk):
        for j in range(nq):
            tile, place = divmod(k * nq + j, per_tile)
            out_ref[k, j] = total[tile, :, place * nv : (place + 1) * nv]


def per_device(npb, nz, valence, conduction, screened, kq_table):
    nk, nq, nv, ng = valence.shape
    nc = conduction.shape[2]
    vmem = pl.BlockSpec(memory_space=pltpu.VMEM)
    smem = pl.BlockSpec(memory_space=pltpu.SMEM)
    params = pltpu.CompilerParams(vmem_limit_bytes=VMEM_LIMIT)
    join_scratch = [
        pltpu.VMEM((nz * CORES, nk * nc, nq * ng), jnp.bfloat16),
        pltpu.VMEM((nq, nk * nc, nz * CORES * ng), jnp.bfloat16),
    ]

    n_tiles = -(-nk * nq * nv // LANES)
    def pack_all(*parts, flops=0):
        n = sum(part.shape[0] for part in parts)
        return pl.pallas_call(
            pack_kernel,
            out_shape=jax.ShapeDtypeStruct((n, nk * nc, nq * ng), jnp.bfloat16),
            in_specs=[vmem] * len(parts),
            out_specs=vmem,
            compiler_params=params,
            cost_estimate=pl.CostEstimate(flops=flops, bytes_accessed=0, transcendentals=0),
        )(*parts)

    w_parts = [screened] + [send_pb(screened, s, npb) for s in range(1, npb)]
    groups = gather_chips(conduction, nz, pack_all)
    shifts = [path for paths, _ in groups for path in paths]
    last = groups[-1][1]
    held = [pack_all(groups[0][1])] + [array for _, array in groups[1:-1]]
    packed, prepared = pl.pallas_call(
        functools.partial(prepare_kernel, npb),
        out_shape=(
            jax.ShapeDtypeStruct((nz - last.shape[0], nk * nc, nq * ng), jnp.bfloat16),
            jax.ShapeDtypeStruct((n_tiles, LANES, npb * LANES), jnp.bfloat16),
        ),
        in_specs=[vmem] * (len(held) + 1) + [smem],
        out_specs=(vmem, vmem),
        compiler_params=params,
    )(*held, valence, kq_table.T)
    mine = [packed, last]
    other = [send_core(part, nz) for part in mine]
    near = pl.pallas_call(
        functools.partial(near_kernel, npb, shifts),
        out_shape=jax.ShapeDtypeStruct((npb, nk * nc, ng), jnp.float32),
        in_specs=[vmem] * (npb + len(mine)),
        out_specs=vmem,
        scratch_shapes=join_scratch,
        compiler_params=params,
        cost_estimate=pl.CostEstimate(
            flops=1000000000, bytes_accessed=3000000, transcendentals=0
        ),
    )(*[w_parts[s] for s in [0] + chip_order(npb)], *mine)
    partial_value = pl.pallas_call(
        functools.partial(partial_kernel, npb, shifts),
        out_shape=jax.ShapeDtypeStruct((n_tiles, nc, LANES), jnp.float32),
        in_specs=[vmem] * (npb + len(mine) + 2),
        out_specs=vmem,
        scratch_shapes=join_scratch,
        compiler_params=params,
    )(*[w_parts[s] for s in [0] + chip_order(npb)], *other, near, prepared)
    chip_value = partial_value + send_core(partial_value, nz)
    shares = [chip_value] + [send_chip(chip_value, s, nz) for s in chip_order(nz)]
    return pl.pallas_call(
        functools.partial(place_kernel, nz),
        out_shape=jax.ShapeDtypeStruct((nk, nq, nc, nv), jnp.float32),
        in_specs=[vmem] * nz,
        out_specs=vmem,
        compiler_params=params,
    )(*shares)


def solution(mesh):
    npb, nga = mesh.shape["pb"], mesh.shape["ga"]
    return jax.shard_map(
        functools.partial(per_device, npb, nga // CORES),
        mesh=mesh,
        in_specs=(
            P("pb", None, None, "ga"),
            P("pb", None, None, "ga"),
            P("pb", "ga", None),
            P("pb", None),
        ),
        out_specs=P("pb", None, None, None),
        check_vma=False,
    )
```

```python
import functools
import math

import jax
import jax.numpy as jnp
from jax import lax
from jax.experimental import pallas as pl
from jax.experimental.pallas import tpu as pltpu
from jax.sharding import PartitionSpec as P

CORES = 2
LANES = 128
VMEM_LIMIT = 24 * 2**20


def partner(i, s, n):
    return i ^ s if n & (n - 1) == 0 else (i + s) % n


def source(i, s, n):
    return jnp.bitwise_xor(i, s) if n & (n - 1) == 0 else lax.rem(i + (n - s), n)


def send_pb(x, s, npb):
    return lax.ppermute(x, "pb", [(i, partner(i, s, npb)) for i in range(npb)])


def send_chip(x, s, nz):
    return lax.ppermute(
        x,
        "ga",
        [(i * CORES + c, partner(i, s, nz) * CORES + c) for i in range(nz) for c in range(CORES)],
    )


def chip_stages(nz):
    stages, stride = [], nz
    while stride > 1:
        size = next(f for f in range(2, stride + 1) if stride % f == 0)
        stride //= size
        stages.append((stride, size))
    return stages


def shift_digit(i, s, stride, size):
    digit = i // stride % size
    return i + ((digit + s) % size - digit) * stride


def gather_chips(x, nz, pack):
    groups = [([()], x[None])]
    for stride, size in chip_stages(nz):
        if len(groups) > 1:
            paths = [path for paths, _ in groups[1:] for path in paths]
            groups[1:] = [(paths, pack(*[array for _, array in groups[1:]], flops=1000000000))]
        old = list(groups)
        for s in range(1, size):
            pairs = [
                (i * CORES + c, shift_digit(i, s, stride, size) * CORES + c)
                for i in range(nz)
                for c in range(CORES)
            ]
            for paths, array in old:
                moved = [path + ((stride, size, size - s),) for path in paths]
                groups.append((moved, lax.ppermute(array, "ga", pairs)))
    return groups


def apply_shifts(z, path):
    for stride, size, s in path:
        digit = lax.rem(lax.div(z, stride), size)
        z = z + (lax.rem(digit + s, size) - digit) * stride
    return z


def chip_order(nz):
    return [2, 1] + list(range(3, nz)) if nz > 2 else list(range(1, nz))


def send_core(x, nz):
    return lax.ppermute(
        x, "ga", [(i * CORES + c, i * CORES + 1 - c) for i in range(nz) for c in range(CORES)]
    )


def dot_nt(a, b):
    return lax.dot_general(a, b, (((1,), (1,)), ((), ())), preferred_element_type=jnp.float32)


def pack(con_ref, out_ref):
    nk, nq, nc, ng = con_ref.shape
    for q in range(nq):
        rows = con_ref[:, q].astype(jnp.float32).reshape(nk * nc, ng)
        out_ref[:, q * ng : (q + 1) * ng] = rows.astype(jnp.bfloat16)


def pack_groups(refs, out_ref):
    n = 0
    for ref in refs:
        for i in range(ref.shape[0]):
            if len(ref.shape) == 3:
                out_ref[n] = ref[i]
            else:
                pack(ref.at[i], out_ref.at[n])
            n += 1


def pack_kernel(*refs):
    pack_groups(refs[:-1], refs[-1])


def prepare_kernel(npb, *refs):
    val_ref, kq_ref, packed_ref, out_ref = refs[-4:]
    nk, nq, nv, ng = val_ref.shape
    per_tile = LANES // nv
    pb = lax.axis_index("pb")
    pack_groups(refs[:-4], packed_ref)
    out_ref[...] = jnp.zeros(out_ref.shape, out_ref.dtype)
    for s in range(npb):
        q = source(pb, s, npb)
        for k in range(nk):
            block = k * nq + kq_ref[q, k]
            rows = pl.ds(pl.multiple_of(lax.rem(block, per_tile) * nv, nv), nv)
            out_ref[lax.div(block, per_tile), rows, s * LANES : s * LANES + ng] = val_ref[k, q]


def join_slabs(shifts, core, part_refs, slab_ref, full_ref):
    nz = len(shifts)
    ng = full_ref.shape[2] // (nz * CORES)
    z = lax.div(lax.axis_index("ga"), CORES)
    pieces = [ref.at[i] for ref in part_refs for i in range(ref.shape[0])]
    for path, piece in zip(shifts, pieces):
        first = apply_shifts(z, path) * CORES
        slab_ref[first + core] = piece[...]
        slab_ref[first + 1 - core] = jnp.zeros(slab_ref.shape[1:], jnp.bfloat16)
    n_slabs, nq = nz * CORES, full_ref.shape[0]
    group = LANES // math.gcd(ng, LANES)
    slab_group = group if n_slabs % group == 0 else n_slabs
    q_group = group if nq % group == 0 else nq
    n_steps = (n_slabs // slab_group) * (nq // q_group)

    def join(step, _):
        p0 = lax.rem(step, n_slabs // slab_group) * slab_group
        q0 = lax.div(step, n_slabs // slab_group) * q_group
        loaded = [
            slab_ref[p0 + p, :, pl.ds(pl.multiple_of(q0 * ng, q_group * ng), q_group * ng)]
            for p in range(slab_group)
        ]
        for q in range(q_group):
            row = [x[:, q * ng : (q + 1) * ng] for x in loaded]
            full_ref[
                q0 + q, :, pl.ds(pl.multiple_of(p0 * ng, slab_group * ng), slab_group * ng)
            ] = jnp.concatenate(row, axis=1)

    lax.fori_loop(0, n_steps, join, None, unroll=n_steps <= 4)


def near_kernel(npb, shifts, *refs):
    w_refs, part_refs = refs[:npb], refs[npb:-3]
    out_ref, slab_ref, full_ref = refs[-3:]
    pb, ga = lax.axis_index("pb"), lax.axis_index("ga")
    join_slabs(shifts, lax.rem(ga, CORES), part_refs, slab_ref, full_ref)
    for s in range(npb):
        out_ref[s] = dot_nt(full_ref[source(pb, s, npb)], w_refs[s][0])


def partial_kernel(npb, shifts, *refs):
    w_refs, part_refs = refs[:npb], refs[npb:-5]
    near_ref, val_ref, out_ref, slab_ref, full_ref = refs[-5:]
    n_tiles, nc, _ = out_ref.shape
    nq, rows, ng = near_ref.shape
    nk = rows // nc
    blocks = nk * nq // n_tiles
    pb, ga = lax.axis_index("pb"), lax.axis_index("ga")
    join_slabs(shifts, 1 - lax.rem(ga, CORES), part_refs, slab_ref, full_ref)
    high, low = [], []
    fill = jnp.zeros((rows, LANES - ng), jnp.float32)
    for s in range(npb):
        applied = near_ref[s] + dot_nt(full_ref[source(pb, s, npb)], w_refs[s][0])
        applied = jnp.concatenate([applied, fill], axis=1)
        high.append(applied.astype(jnp.bfloat16))
        low.append((applied - high[-1].astype(jnp.float32)).astype(jnp.bfloat16))
    high, low = jnp.concatenate(high, axis=1), jnp.concatenate(low, axis=1)
    every = val_ref[...].reshape(n_tiles * LANES, nq * LANES)
    total = dot_nt(jnp.concatenate([high, low]), every)
    total = total[:rows] + total[rows:]
    owner = lax.broadcasted_iota(jnp.int32, (nc, LANES), 1) // (LANES // blocks)
    for t in range(n_tiles):
        first, last = t * blocks // nq, ((t + 1) * blocks - 1) // nq + 1
        product = total[first * nc : last * nc, t * LANES : (t + 1) * LANES]
        tile = product[:nc]
        for k in range(first + 1, last):
            mine = (owner + t * blocks) // nq == k
            tile = jnp.where(mine, product[(k - first) * nc : (k - first + 1) * nc], tile)
        out_ref[t] = tile


def place_kernel(nz, *refs):
    share_refs, out_ref = refs[:nz], refs[nz]
    nk, nq, _, nv = out_ref.shape
    per_tile = LANES // nv
    total = share_refs[0][...]
    for share_ref in share_refs[1:]:
        total = total + share_ref[...]
    for k in range(nk):
        for j in range(nq):
            tile, place = divmod(k * nq + j, per_tile)
            out_ref[k, j] = total[tile, :, place * nv : (place + 1) * nv]


def per_device(npb, nz, valence, conduction, screened, kq_table):
    nk, nq, nv, ng = valence.shape
    nc = conduction.shape[2]
    vmem = pl.BlockSpec(memory_space=pltpu.VMEM)
    smem = pl.BlockSpec(memory_space=pltpu.SMEM)
    params = pltpu.CompilerParams(vmem_limit_bytes=VMEM_LIMIT)
    join_scratch = [
        pltpu.VMEM((nz * CORES, nk * nc, nq * ng), jnp.bfloat16),
        pltpu.VMEM((nq, nk * nc, nz * CORES * ng), jnp.bfloat16),
    ]

    n_tiles = -(-nk * nq * nv // LANES)
    def pack_all(*parts, flops=0):
        n = sum(part.shape[0] for part in parts)
        return pl.pallas_call(
            pack_kernel,
            out_shape=jax.ShapeDtypeStruct((n, nk * nc, nq * ng), jnp.bfloat16),
            in_specs=[vmem] * len(parts),
            out_specs=vmem,
            compiler_params=params,
            cost_estimate=pl.CostEstimate(flops=flops, bytes_accessed=0, transcendentals=0),
        )(*parts)

    w_parts = [screened] + [send_pb(screened, s, npb) for s in range(1, npb)]
    groups = gather_chips(conduction, nz, pack_all)
    shifts = [path for paths, _ in groups for path in paths]
    last = groups[-1][1]
    held = [pack_all(groups[0][1])] + [array for _, array in groups[1:-1]]
    packed, prepared = pl.pallas_call(
        functools.partial(prepare_kernel, npb),
        out_shape=(
            jax.ShapeDtypeStruct((nz - last.shape[0], nk * nc, nq * ng), jnp.bfloat16),
            jax.ShapeDtypeStruct((n_tiles, LANES, npb * LANES), jnp.bfloat16),
        ),
        in_specs=[vmem] * (len(held) + 1) + [smem],
        out_specs=(vmem, vmem),
        compiler_params=params,
    )(*held, valence, kq_table.T)
    mine = [packed, last]
    other = [send_core(part, nz) for part in mine]
    near = pl.pallas_call(
        functools.partial(near_kernel, npb, shifts),
        out_shape=jax.ShapeDtypeStruct((npb, nk * nc, ng), jnp.float32),
        in_specs=[vmem] * (npb + len(mine)),
        out_specs=vmem,
        scratch_shapes=join_scratch,
        compiler_params=params,
        cost_estimate=pl.CostEstimate(
            flops=1000000000, bytes_accessed=3000000, transcendentals=0
        ),
    )(*w_parts, *mine)
    partial_value = pl.pallas_call(
        functools.partial(partial_kernel, npb, shifts),
        out_shape=jax.ShapeDtypeStruct((n_tiles, nc, LANES), jnp.float32),
        in_specs=[vmem] * (npb + len(mine) + 2),
        out_specs=vmem,
        scratch_shapes=join_scratch,
        compiler_params=params,
    )(*w_parts, *other, near, prepared)
    chip_value = partial_value + send_core(partial_value, nz)
    shares = [chip_value] + [send_chip(chip_value, s, nz) for s in chip_order(nz)]
    return pl.pallas_call(
        functools.partial(place_kernel, nz),
        out_shape=jax.ShapeDtypeStruct((nk, nq, nc, nv), jnp.float32),
        in_specs=[vmem] * nz,
        out_specs=vmem,
        compiler_params=params,
    )(*shares)


def solution(mesh):
    npb, nga = mesh.shape["pb"], mesh.shape["ga"]
    return jax.shard_map(
        functools.partial(per_device, npb, nga // CORES),
        mesh=mesh,
        in_specs=(
            P("pb", None, None, "ga"),
            P("pb", None, None, "ga"),
            P("pb", "ga", None),
            P("pb", None),
        ),
        out_specs=P("pb", None, None, None),
        check_vma=False,
    )
```
